32 devices in a mesh: skyy: 4 (over x, core), skyx: 8 (over z, y).
Axes of the slice: x: 2, y: 2, z: 4, core: 2. Of those that a mesh axis runs over, the one named last changes fastest.
Arguments:
- tiles: bfloat16 [4, 64, 256, 256], P('skyy', 'skyx'), may hold values from -6 to 6
- coeffs: bfloat16 [4, 64, 5, 256, 256], P('skyy', 'skyx'), may hold values from -4 to 4
- weights: bfloat16 [4, 64], P('skyy', 'skyx'), may hold values from 0.25 to 4
- tile_slot: int32 [4, 64], P('skyy', 'skyx'), may hold values from 0 to 15, as said below
- slot_offset: int32 [2, 4, 128], P(None, 'skyy', 'skyx'), may hold values from -224 to 480
Outputs:
- coadd: float32 [2048, 4096], P('skyy', 'skyx')
- detection: float32 [2048, 4096], P('skyy', 'skyx')
The draws below stay inside these ranges and needn't reach their ends.
Inputs may be any that keep to these rules, and one draw needn't show every extreme that they name: `tile_slot`: within one device the values are distinct; each device sends at most 2 tiles to one patch, and in every row of patches one patch receives 2 tiles from every device of that row.
All inputs are finite; a program needn't handle non-finite values.
Results may differ from the reference program's by a relative error of at most 0.013.
Values may be sent and summed in bfloat16 or wider, within the bound.
A program may use at most 192 MiB of HBM per device.

```python
import math
import jax
import jax.numpy as jnp
from jax import lax

TILE = 256
NB = 5
REACH = 10
CAP = 2
PATCH = 512
V_DEV = 8
SLOTS = 16
N_SKYY = 4
N_SKYX = 8


def draw_tile_slot(key, part):
    slots = N_SKYX * CAP
    hot = jax.random.randint(jax.random.fold_in(key, 7), (N_SKYY,), 0, N_SKYX)
    scores = jax.random.randint(jax.random.fold_in(key, 11), (N_SKYY, N_SKYX, slots), 0, 1 << 20)
    index = jnp.arange(slots, dtype=jnp.int32)
    scores = scores * slots + index[None, None, :]
    is_hot = index[None, None, :] // CAP == hot[:, None, None]
    scores = jnp.where(is_hot, -1 - index[None, None, :], scores)
    order = jnp.argsort(scores, axis=-1, stable=True)
    return order[:, :, :V_DEV].reshape(N_SKYY, N_SKYX * V_DEV).astype(jnp.int32)


def set_ends(values, stream_key, least, top_value):
    index_at = [jax.random.randint(jax.random.fold_in(stream_key, axis), (), 0, length) for axis, length in enumerate(values.shape)]
    main_axis = values.shape.index(max(values.shape))
    neighbour = index_at[:main_axis] + [(index_at[main_axis] + 1) % values.shape[main_axis]] + index_at[main_axis + 1:]
    return values.at[tuple(index_at)].set(least).at[tuple(neighbour)].set(top_value)


def shard_levels(rng, shape, shards, smallest, high):
    loudness = 1.0
    for dim, parts in shards:
        heights = jax.random.uniform(jax.random.fold_in(jax.random.fold_in(rng, 6), dim), (parts,), jnp.float32, smallest / len(shards), high / len(shards))
        loudness = loudness * jnp.repeat(jnp.exp(heights), shape[dim] // parts).reshape((-1,) + (1,) * (len(shape) - 1 - dim))
    return loudness


def bell_draw(rng, shape, scale, most, split=(), held_as=jnp.bfloat16):
    loudness = shard_levels(rng, shape, split, -0.22, 0.18) if split else 1.0
    entries = jax.random.normal(rng, shape, jnp.float32) * scale * loudness
    return jnp.minimum(jnp.maximum(entries, -most), most).astype(held_as)


def setup_inputs(seed: int = 0) -> dict:
    key_list = jax.random.split(jax.random.key(seed), 6)
    return {
        "tiles": bell_draw(key_list[0], (N_SKYY, N_SKYX * V_DEV, TILE, TILE), 1.0, 6.0, ((0, 4), (1, 8))),
        "coeffs": bell_draw(key_list[1], (N_SKYY, N_SKYX * V_DEV, NB, TILE, TILE), 0.6, 4.0, ((0, 4), (1, 8))),
        "weights": jnp.clip(jnp.exp(math.log(4.0) - 2.7725887 * jax.random.uniform(key_list[2], (N_SKYY, N_SKYX * V_DEV), jnp.float32) ** shard_levels(key_list[2], (N_SKYY, N_SKYX * V_DEV), ((0, 4), (1, 8)), -0.2, 0.2)), 0.25, 4.0).astype(jnp.bfloat16),
        "tile_slot": draw_tile_slot(jax.random.fold_in(key_list[5], 71), 0),
        "slot_offset": set_ends(jax.random.randint(key_list[4], (2, N_SKYY, N_SKYX * SLOTS), -(TILE - TILE // 8), PATCH - TILE // 8 + 1), jax.random.fold_in(key_list[4], 1), -(TILE - TILE // 8), (PATCH - TILE // 8 + 1) - 1).astype(jnp.int32),
    }


basis_widths = (1.0, 1.8, 2.6, 3.6, 5.0)
detect_width = 2.5


def band_matrices(size):
    rows = jnp.arange(size, dtype=jnp.int32)[:, None]
    cols = jnp.arange(size, dtype=jnp.int32)[None, :]
    gap = (cols - rows).astype(jnp.float32)
    inside = jnp.abs(cols - rows) <= REACH
    taps = jnp.arange(-REACH, REACH + 1).astype(jnp.float32)
    mats = []
    for width in basis_widths:
        total = jnp.sum(jnp.exp(-taps * taps / (2.0 * width * width)))
        mats.append(jnp.where(inside, jnp.exp(-gap * gap / (2.0 * width * width)) / total, 0.0))
    return jnp.stack(mats).astype(jnp.bfloat16)


def match_tile(tile, coeff, basis):
    high = lax.Precision.HIGHEST
    vert = jnp.einsum('bij,jk->bik', basis.astype(jnp.float32), tile.astype(jnp.float32), precision=high).astype(jnp.bfloat16)
    horiz = jnp.einsum('bik,bjk->bij', vert.astype(jnp.float32), basis.astype(jnp.float32), precision=high)
    result = jnp.sum(coeff.astype(jnp.float32) * horiz, axis=0).astype(jnp.bfloat16)
    return lax.optimization_barrier(result)


def coadd_patch(matched, slot_weight, offsets):
    size = matched.shape[1]
    canvas = PATCH + 2 * size
    zero_canvas = jnp.zeros((canvas, canvas), jnp.float32)

    def add_one(index, carry):
        numer, cover = carry
        row = offsets[0, index] + size
        col = offsets[1, index] + size
        weight = slot_weight[index].astype(jnp.float32)
        region = lax.dynamic_slice(numer, (row, col), (size, size))
        numer = lax.dynamic_update_slice(numer, region + weight * matched[index].astype(jnp.float32), (row, col))
        footprint = lax.dynamic_slice(cover, (row, col), (size, size))
        cover = lax.dynamic_update_slice(cover, footprint + weight, (row, col))
        return numer, cover

    numer, cover = lax.fori_loop(0, matched.shape[0], add_one, (zero_canvas, zero_canvas))
    numer = numer[size:size + PATCH, size:size + PATCH]
    cover = cover[size:size + PATCH, size:size + PATCH]
    return numer / (1.0 + cover)


def detect(extended, out_rows, out_cols):
    taps = jnp.arange(-REACH, REACH + 1).astype(jnp.float32)
    kernel = jnp.exp(-taps * taps / (2.0 * detect_width * detect_width))
    kernel = kernel / jnp.sum(kernel)
    vert = jnp.zeros((out_rows, extended.shape[1]), jnp.float32)
    for step in range(2 * REACH + 1):
        vert = vert + kernel[step] * extended[step:step + out_rows, :]
    result = jnp.zeros((out_rows, out_cols), jnp.float32)
    for step in range(2 * REACH + 1):
        result = result + kernel[step] * vert[:, step:step + out_cols]
    return result


def reference(tiles, coeffs, weights, tile_slot, slot_offset):
    slots = N_SKYX * CAP
    basis = band_matrices(TILE)
    patch_rows = []
    for sky_row in range(N_SKYY):
        matched = lax.map(lambda pair: match_tile(pair[0], pair[1], basis), (tiles[sky_row], coeffs[sky_row]))
        owner_slot = tile_slot[sky_row].reshape(N_SKYX, V_DEV)
        hits = owner_slot[:, :, None] == jnp.arange(slots, dtype=jnp.int32)[None, None, :]
        present = jnp.any(hits, axis=1)
        which = jnp.sum(jnp.where(hits, jnp.arange(V_DEV, dtype=jnp.int32)[None, :, None], 0), axis=1).astype(jnp.int32)
        source = (jnp.arange(N_SKYX, dtype=jnp.int32)[:, None] * V_DEV + which).astype(jnp.int32)
        row_weight = weights[sky_row]
        row_offsets = slot_offset[:, sky_row, :]

        def one_patch(column):
            start = (column * CAP).astype(jnp.int32)
            pick = lax.dynamic_slice_in_dim(source, start, CAP, 1).reshape(-1)
            live = lax.dynamic_slice_in_dim(present, start, CAP, 1).reshape(-1)
            slot_tiles = matched[pick]
            slot_weight = jnp.where(live, row_weight[pick], jnp.zeros((), jnp.bfloat16))
            offsets = lax.dynamic_slice_in_dim(row_offsets, (column * slots).astype(jnp.int32), slots, 1)
            return coadd_patch(slot_tiles, slot_weight, offsets)

        patch_rows.append(lax.map(one_patch, jnp.arange(N_SKYX, dtype=jnp.int32)))
    patches = jnp.stack(patch_rows)
    coadd = patches.transpose(0, 2, 1, 3).reshape(N_SKYY * PATCH, N_SKYX * PATCH)
    padded = jnp.pad(coadd, REACH)
    detection = detect(padded, coadd.shape[0], coadd.shape[1])
    return coadd, detection
```

```python
import functools

import jax
import jax.numpy as jnp
import numpy as np
from jax import lax
from jax.experimental import pallas as pl
from jax.experimental.pallas import tpu as pltpu
from jax.sharding import PartitionSpec as P

NB = 5
REACH = 10
CAP = 2
PATCH = 512
EDGE = 16
LANES = 128

basis_widths = (1.0, 1.8, 2.6, 3.6, 5.0)
detect_width = 2.5
MESH = pl.DeviceIdType.MESH


def band_matrices(size):
    rows = np.arange(size)[:, None]
    cols = np.arange(size)[None, :]
    gap = (cols - rows).astype(np.float32)
    inside = np.abs(cols - rows) <= REACH
    taps = np.arange(-REACH, REACH + 1).astype(np.float32)
    mats = []
    for width in basis_widths:
        total = np.sum(np.exp(-taps * taps / np.float32(2.0 * width * width)))
        mats.append(np.where(inside, np.exp(-gap * gap / np.float32(2.0 * width * width)) / total, 0.0))
    return np.concatenate(mats).astype(jnp.bfloat16)


def detect_matrix(positions, size):
    taps = np.arange(-REACH, REACH + 1).astype(np.float32)
    total = np.sum(np.exp(-taps * taps / np.float32(2.0 * detect_width * detect_width)))
    gap = np.asarray(positions)[:, None] - np.arange(size)[None, :]
    value = np.exp(-(gap * gap).astype(np.float32) / np.float32(2.0 * detect_width * detect_width)) / total
    return np.where(np.abs(gap) <= REACH, value, 0.0).astype(jnp.bfloat16)


def dot(a, b):
    return jnp.dot(a, b, preferred_element_type=jnp.float32)


def dot_t(a, b):
    return lax.dot_general(a, b, (((1,), (1,)), ((), ())), preferred_element_type=jnp.float32)


def dot_0(a, b):
    return lax.dot_general(a, b, (((0,), (0,)), ((), ())), preferred_element_type=jnp.float32)


def kernel(
    rows, n,
    which, wslot, offs,
    tiles_hbm, coeffs_hbm, basis, gmid, gedge, gedge_t, gcorner, pick,
    coadd_hbm, detect_hbm,
    tiles, coeffs, send, recv, wsend, wrecv, numer, result, rowcov, colcov,
    cb, vhalo, hsend, hhalo, corner, local_sem,
    send_sem, recv_sem, wsend_sem, wrecv_sem, hsend_sem, hrecv_sem,
):
    row, me = lax.axis_index("skyy"), lax.axis_index("skyx")
    size = tiles.shape[1]
    patch = numer.shape[0]
    f32, bf16 = jnp.float32, jnp.bfloat16

    load_tiles = pltpu.make_async_copy(tiles_hbm, tiles, local_sem.at[0])
    load_coeffs = pltpu.make_async_copy(coeffs_hbm, coeffs, local_sem.at[1])
    load_tiles.start()
    load_coeffs.start()

    vhalo[...] = jnp.zeros_like(vhalo)
    hhalo[...] = jnp.zeros_like(hhalo)
    corner[...] = jnp.zeros_like(corner)

    up, down, left, right = row > 0, row < rows - 1, me > 0, me < n - 1
    both = jnp.logical_and
    moves = [
        (0, up, -1, 0, lambda: cb.at[pl.ds(0, EDGE), :], lambda: vhalo.at[pl.ds(EDGE, EDGE), :]),
        (1, down, 1, 0, lambda: cb.at[pl.ds(patch - EDGE, EDGE), :], lambda: vhalo.at[pl.ds(0, EDGE), :]),
        (2, left, 0, -1, lambda: hsend.at[pl.ds(0, EDGE), :], lambda: hhalo.at[pl.ds(EDGE, EDGE), :]),
        (3, right, 0, 1, lambda: hsend.at[pl.ds(EDGE, EDGE), :], lambda: hhalo.at[pl.ds(0, EDGE), :]),
        (4, both(up, left), -1, -1, lambda: cb.at[pl.ds(0, EDGE), pl.ds(0, LANES)],
         lambda: corner.at[pl.ds(EDGE, EDGE), pl.ds(LANES, LANES)]),
        (5, both(up, right), -1, 1, lambda: cb.at[pl.ds(0, EDGE), pl.ds(patch - LANES, LANES)],
         lambda: corner.at[pl.ds(EDGE, EDGE), pl.ds(0, LANES)]),
        (6, both(down, left), 1, -1, lambda: cb.at[pl.ds(patch - EDGE, EDGE), pl.ds(0, LANES)],
         lambda: corner.at[pl.ds(0, EDGE), pl.ds(LANES, LANES)]),
        (7, both(down, right), 1, 1, lambda: cb.at[pl.ds(patch - EDGE, EDGE), pl.ds(patch - LANES, LANES)],
         lambda: corner.at[pl.ds(0, EDGE), pl.ds(0, LANES)]),
    ]
    opposite = {0: 1, 1: 0, 2: 3, 3: 2, 4: 7, 5: 6, 6: 5, 7: 4}

    barrier = pltpu.get_barrier_semaphore()

    def greet(d, carry):
        pl.semaphore_signal(barrier, inc=1, device_id={"skyx": lax.rem(me + d, n)}, device_id_type=MESH)
        return carry

    lax.fori_loop(1, n, greet, 0)
    expected = n - 1
    for index, exists, dy, dx, _, _ in moves:
        if dy != 0:
            @pl.when(exists)
            def _(dy=dy, dx=dx):
                pl.semaphore_signal(
                    barrier, inc=1, device_id={"skyy": row + dy, "skyx": me + dx}, device_id_type=MESH
                )
            expected = expected + jnp.where(exists, 1, 0)
    pl.semaphore_wait(barrier, expected)

    def weight_copy(d):
        return pltpu.make_async_remote_copy(
            src_ref=wsend.at[d], dst_ref=wrecv.at[d],
            send_sem=wsend_sem.at[d], recv_sem=wrecv_sem.at[d],
            device_id={"skyx": lax.rem(me + d, n)}, device_id_type=MESH,
        )

    line = lax.broadcasted_iota(jnp.int32, (8, LANES), 0)

    def weight_block(column):
        return jnp.where(line == 0, wslot[column * CAP], wslot[column * CAP + 1])

    def send_weight(d, carry):
        wsend[d] = weight_block(lax.rem(me + d, n))
        weight_copy(d).start()
        return carry

    wrecv[0] = weight_block(me)
    lax.fori_loop(1, n, send_weight, 0)

    def match(index):
        x = tiles[index]
        vert = dot(basis[...], x).astype(bf16)
        total = jnp.zeros((size, size), f32)
        for b in range(NB):
            part = slice(b * size, (b + 1) * size)
            total += coeffs[index, b].astype(f32) * dot(vert[part], basis[part, :])
        return total.astype(bf16)

    def tile_copy(j, d):
        return pltpu.make_async_remote_copy(
            src_ref=send.at[j], dst_ref=recv.at[j],
            send_sem=send_sem.at[j], recv_sem=recv_sem.at[j],
            device_id={"skyx": lax.rem(me + d, n)}, device_id_type=MESH,
        )

    def distance(step):
        t = step // CAP
        odd = lax.rem(t, 2)
        return n // 2 + ((t + 1) // 2) * (2 * odd - 1)

    load_tiles.wait()
    load_coeffs.wait()

    def send_one(step, carry):
        d = distance(step)
        s = lax.rem(step, CAP)
        j = d * CAP + s
        send[j] = match(which[lax.rem(me + d, n) * CAP + s])
        tile_copy(j, d).start()
        return carry

    steps = CAP * (n - 1)
    lax.fori_loop(0, steps, send_one, 0)

    def own(s, carry):
        recv[s] = match(which[me * CAP + s])
        return carry

    lax.fori_loop(0, CAP, own, 0)

    numer[...] = jnp.zeros_like(numer)

    def weight_in(d, carry):
        copy = weight_copy(d)
        copy.wait_recv()
        copy.wait_send()
        return carry

    lax.fori_loop(1, n, weight_in, 0)

    pixel = lax.broadcasted_iota(jnp.int32, (1, patch), 1)

    def place(j, d):
        s = lax.rem(j, CAP)
        slot = lax.rem(me - d + n, n) * CAP + s
        oy, ox = offs[0, slot], offs[1, slot]
        w = wrecv[d, pl.ds(s, 1), :]
        w = jnp.concatenate([w] * (patch // LANES), axis=1)
        rowcov[pl.ds(j, 1), :] = jnp.where((pixel >= oy) & (pixel < oy + size), 1.0, 0.0)
        colcov[pl.ds(j, 1), :] = jnp.where((pixel >= ox) & (pixel < ox + size), w, 0.0)
        r = lax.broadcasted_iota(jnp.int32, (patch, size), 0) - lax.broadcasted_iota(jnp.int32, (patch, size), 1)
        rowhit = jnp.where(r == oy, 1.0, 0.0).astype(bf16)
        c = lax.broadcasted_iota(jnp.int32, (size, patch), 1) - lax.broadcasted_iota(jnp.int32, (size, patch), 0)
        colhit = jnp.where(c == ox, w, 0.0).astype(bf16)
        placed = dot(rowhit, recv[j]).astype(bf16)
        numer[...] += dot(placed, colhit)

    def place_own(s, carry):
        place(s, 0)
        return carry

    lax.fori_loop(0, CAP, place_own, 0)

    def place_one(step, carry):
        d = distance(step)
        j = d * CAP + lax.rem(step, CAP)
        tile_copy(j, d).wait_recv()
        place(j, d)
        return carry

    lax.fori_loop(0, steps, place_one, 0)

    cover = dot_0(rowcov[...].astype(bf16), colcov[...].astype(bf16))
    coadd = numer[...] / (1.0 + cover)
    numer[...] = coadd
    cb[...] = coadd.astype(bf16)
    hsend[...] = dot_t(pick[...], cb[...]).astype(bf16)

    def halo_copy(move):
        index, _, dy, dx, src, dst = move
        return pltpu.make_async_remote_copy(
            src_ref=src(), dst_ref=dst(),
            send_sem=hsend_sem.at[index], recv_sem=hrecv_sem.at[index],
            device_id={"skyy": row + dy, "skyx": me + dx}, device_id_type=MESH,
        )

    for move in moves:
        @pl.when(move[1])
        def _(move=move):
            halo_copy(move).start()

    store_coadd = pltpu.make_async_copy(numer, coadd_hbm, local_sem.at[2])
    store_coadd.start()

    vert = dot(gmid[...], cb[...])

    def drain(step, carry):
        d = distance(step)
        tile_copy(d * CAP + lax.rem(step, CAP), d).wait_send()
        return carry

    lax.fori_loop(0, steps, drain, 0)

    for move in moves:
        @pl.when(moves[opposite[move[0]]][1])
        def _(move=move):
            halo_copy(move).wait_recv()

    vert = (vert + dot(gedge_t[...], vhalo[...])).astype(bf16)
    sides = dot_t(gmid[...], hhalo[...]).astype(bf16)
    ends = dot(gedge_t[...], corner[...]).astype(bf16)
    result[...] = dot(vert, gmid[...]) + dot(sides, gedge[...]) + dot(ends, gcorner[...])
    store_result = pltpu.make_async_copy(result, detect_hbm, local_sem.at[3])
    store_result.start()
    for move in moves:
        @pl.when(move[1])
        def _(move=move):
            halo_copy(move).wait_send()
    store_coadd.wait()
    store_result.wait()


def body(rows, n, tiles, coeffs, weights, tile_slot, slot_offset):
    count, size = tiles.shape[1], tiles.shape[2]
    slots = n * CAP
    patch = PATCH
    f32, bf16 = jnp.float32, jnp.bfloat16
    hits = tile_slot[0][:, None] == jnp.arange(slots, dtype=jnp.int32)[None, :]
    which = jnp.sum(jnp.where(hits, jnp.arange(count, dtype=jnp.int32)[:, None], 0), axis=0)
    wslot = jnp.sum(jnp.where(hits, weights[0].astype(f32)[:, None], 0.0), axis=0)

    basis = jnp.asarray(band_matrices(size))
    gmid = jnp.asarray(detect_matrix(np.arange(patch), patch))
    edge_at = np.concatenate([np.arange(-EDGE, 0), np.arange(patch, patch + EDGE)])
    gedge_np = detect_matrix(edge_at, patch)
    corner_at = np.concatenate([np.arange(-LANES, 0), np.arange(patch, patch + LANES)])
    gcorner = jnp.asarray(detect_matrix(corner_at, patch))
    pick_at = np.concatenate([np.arange(EDGE), np.arange(patch - EDGE, patch)])
    pick = jnp.asarray((pick_at[:, None] == np.arange(patch)[None, :]).astype(jnp.bfloat16))

    smem = pl.BlockSpec(memory_space=pltpu.SMEM)
    vmem = pl.BlockSpec(memory_space=pltpu.VMEM)
    anyspace = pl.BlockSpec(memory_space=pl.ANY)
    dma = pltpu.SemaphoreType.DMA
    return pl.pallas_call(
        functools.partial(kernel, rows, n),
        out_shape=[jax.ShapeDtypeStruct((patch, patch), f32)] * 2,
        in_specs=[smem] * 3 + [anyspace] * 2 + [vmem] * 6,
        out_specs=[anyspace] * 2,
        scratch_shapes=[
            pltpu.VMEM((count, size, size), bf16),
            pltpu.VMEM((count, NB, size, size), bf16),
            pltpu.VMEM((slots, size, size), bf16),
            pltpu.VMEM((slots, size, size), bf16),
            pltpu.VMEM((n, 8, LANES), f32),
            pltpu.VMEM((n, 8, LANES), f32),
            pltpu.VMEM((patch, patch), f32),
            pltpu.VMEM((patch, patch), f32),
            pltpu.VMEM((slots, patch), f32),
            pltpu.VMEM((slots, patch), f32),
            pltpu.VMEM((patch, patch), bf16),
            pltpu.VMEM((2 * EDGE, patch), bf16),
            pltpu.VMEM((2 * EDGE, patch), bf16),
            pltpu.VMEM((2 * EDGE, patch), bf16),
            pltpu.VMEM((2 * EDGE, 2 * LANES), bf16),
            dma((4,)),
            dma((slots,)),
            dma((slots,)),
            dma((n,)),
            dma((n,)),
            dma((8,)),
            dma((8,)),
        ],
        compiler_params=pltpu.CompilerParams(
            collective_id=0, has_side_effects=True, vmem_limit_bytes=44 * 1024 * 1024
        ),
        name="coadd",
    )(
        which, wslot, slot_offset[:, 0, :],
        tiles[0], coeffs[0], basis, gmid, jnp.asarray(gedge_np), jnp.asarray(gedge_np.T.copy()), gcorner, pick,
    )


def solution(mesh):
    in_specs = (
        P("skyy", "skyx", None, None),
        P("skyy", "skyx", None, None, None),
        P("skyy", "skyx"),
        P("skyy", "skyx"),
        P(None, "skyy", "skyx"),
    )
    out_specs = (P("skyy", "skyx"), P("skyy", "skyx"))
    return jax.shard_map(
        functools.partial(body, mesh.shape["skyy"], mesh.shape["skyx"]),
        mesh=mesh, in_specs=in_specs, out_specs=out_specs, check_vma=False,
    )
```

```python
import functools

import jax
import jax.numpy as jnp
import numpy as np
from jax import lax
from jax.experimental import pallas as pl
from jax.experimental.pallas import tpu as pltpu
from jax.sharding import PartitionSpec as P

NB = 5
REACH = 10
CAP = 2
PATCH = 512
EDGE = 16
LANES = 128
VMEM_LIMIT = 63 * 1024 * 1024

basis_widths = (1.0, 1.8, 2.6, 3.6, 5.0)
detect_width = 2.5
MESH = pl.DeviceIdType.MESH


def band_matrices(size):
    rows = np.arange(size)[:, None]
    cols = np.arange(size)[None, :]
    gap = (cols - rows).astype(np.float32)
    inside = np.abs(cols - rows) <= REACH
    taps = np.arange(-REACH, REACH + 1).astype(np.float32)
    mats = []
    for width in basis_widths:
        total = np.sum(np.exp(-taps * taps / np.float32(2.0 * width * width)))
        mats.append(np.where(inside, np.exp(-gap * gap / np.float32(2.0 * width * width)) / total, 0.0))
    return np.concatenate(mats).astype(jnp.bfloat16)


def detect_matrix(positions, size):
    taps = np.arange(-REACH, REACH + 1).astype(np.float32)
    total = np.sum(np.exp(-taps * taps / np.float32(2.0 * detect_width * detect_width)))
    gap = np.asarray(positions)[:, None] - np.arange(size)[None, :]
    value = np.exp(-(gap * gap).astype(np.float32) / np.float32(2.0 * detect_width * detect_width)) / total
    return np.where(np.abs(gap) <= REACH, value, 0.0).astype(jnp.bfloat16)


def dot(a, b):
    return jnp.dot(a, b, preferred_element_type=jnp.float32)


def dot_t(a, b):
    return lax.dot_general(a, b, (((1,), (1,)), ((), ())), preferred_element_type=jnp.float32)


def dot_0(a, b):
    return lax.dot_general(a, b, (((0,), (0,)), ((), ())), preferred_element_type=jnp.float32)


def kernel(
    rows, n,
    slot_at, offs, slot_row, weight_row,
    tiles_hbm, coeffs_hbm, basis_hbm, bands_hbm,
    coadd_hbm, detect_hbm,
    tiles, coeffs, basis, bands, send, recv, wsend, wrecv, numer, result, rowcov, colcov,
    cb, vhalo, hsend, hhalo, corner, local_sem,
    send_sem, recv_sem, wsend_sem, wrecv_sem, hsend_sem, hrecv_sem,
):
    row, me = lax.axis_index("skyy"), lax.axis_index("skyx")
    size = tiles.shape[1]
    patch = numer.shape[0]
    f32, bf16 = jnp.float32, jnp.bfloat16

    load_tiles = pltpu.make_async_copy(tiles_hbm, tiles, local_sem.at[0])
    load_coeffs = pltpu.make_async_copy(coeffs_hbm, coeffs, local_sem.at[1])
    load_basis = pltpu.make_async_copy(basis_hbm, basis, local_sem.at[4])
    load_bands = pltpu.make_async_copy(bands_hbm, bands, local_sem.at[5])
    load_tiles.start()
    load_basis.start()
    load_coeffs.start()
    load_bands.start()
    gmid = bands.at[pl.ds(0, patch), :]
    gcorner = bands.at[pl.ds(patch, 2 * LANES), :]
    gedge = bands.at[pl.ds(patch + 2 * LANES, 2 * EDGE), :]
    pick = bands.at[pl.ds(patch + 2 * LANES + 2 * EDGE, 2 * EDGE), :]

    vhalo[...] = jnp.zeros_like(vhalo)
    hhalo[...] = jnp.zeros_like(hhalo)
    corner[...] = jnp.zeros_like(corner)

    up, down, left, right = row > 0, row < rows - 1, me > 0, me < n - 1
    both = jnp.logical_and
    moves = [
        (0, up, -1, 0, lambda: cb.at[pl.ds(0, EDGE), :], lambda: vhalo.at[pl.ds(EDGE, EDGE), :]),
        (1, down, 1, 0, lambda: cb.at[pl.ds(patch - EDGE, EDGE), :], lambda: vhalo.at[pl.ds(0, EDGE), :]),
        (2, left, 0, -1, lambda: hsend.at[pl.ds(0, EDGE), :], lambda: hhalo.at[pl.ds(EDGE, EDGE), :]),
        (3, right, 0, 1, lambda: hsend.at[pl.ds(EDGE, EDGE), :], lambda: hhalo.at[pl.ds(0, EDGE), :]),
        (4, both(up, left), -1, -1, lambda: cb.at[pl.ds(0, EDGE), pl.ds(0, LANES)],
         lambda: corner.at[pl.ds(EDGE, EDGE), pl.ds(LANES, LANES)]),
        (5, both(up, right), -1, 1, lambda: cb.at[pl.ds(0, EDGE), pl.ds(patch - LANES, LANES)],
         lambda: corner.at[pl.ds(EDGE, EDGE), pl.ds(0, LANES)]),
        (6, both(down, left), 1, -1, lambda: cb.at[pl.ds(patch - EDGE, EDGE), pl.ds(0, LANES)],
         lambda: corner.at[pl.ds(0, EDGE), pl.ds(LANES, LANES)]),
        (7, both(down, right), 1, 1, lambda: cb.at[pl.ds(patch - EDGE, EDGE), pl.ds(patch - LANES, LANES)],
         lambda: corner.at[pl.ds(0, EDGE), pl.ds(0, LANES)]),
    ]
    opposite = {0: 1, 1: 0, 2: 3, 3: 2, 4: 7, 5: 6, 6: 5, 7: 4}

    barrier = pltpu.get_barrier_semaphore()

    def greet(d, carry):
        pl.semaphore_signal(barrier, inc=1, device_id={"skyx": lax.rem(me + d, n)}, device_id_type=MESH)
        return carry

    lax.fori_loop(1, n, greet, 0)
    expected = n - 1
    for index, exists, dy, dx, _, _ in moves:
        if dy != 0:
            @pl.when(exists)
            def _(dy=dy, dx=dx):
                pl.semaphore_signal(
                    barrier, inc=1, device_id={"skyy": row + dy, "skyx": me + dx}, device_id_type=MESH
                )
            expected = expected + jnp.where(exists, 1, 0)
    pl.semaphore_wait(barrier, expected)

    def weight_copy(d):
        return pltpu.make_async_remote_copy(
            src_ref=wsend.at[d], dst_ref=wrecv.at[d],
            send_sem=wsend_sem.at[d], recv_sem=wrecv_sem.at[d],
            device_id={"skyx": lax.rem(me + d, n)}, device_id_type=MESH,
        )

    line = lax.broadcasted_iota(jnp.int32, (8, LANES), 0)

    weight_of = weight_row[...].astype(f32)
    count = tiles.shape[0]

    def slot_weight(slot):
        return jnp.sum(jnp.where(slot_row[...] == slot, weight_of, 0.0), axis=1, keepdims=True)

    def weight_block(column):
        return jnp.where(line == 0, slot_weight(column * CAP), slot_weight(column * CAP + 1))

    def which(slot):
        index = jnp.int32(0)
        for m in range(count):
            index = jnp.where(slot_at[0, m] == slot, m, index)
        return index

    def send_weight(d, carry):
        wsend[d] = weight_block(lax.rem(me + d, n))
        weight_copy(d).start()
        return carry

    wrecv[0] = weight_block(me)
    lax.fori_loop(1, n, send_weight, 0)

    def match(index):
        x = tiles[index]
        vert = dot(basis[...], x).astype(bf16)
        total = jnp.zeros((size, size), f32)
        for b in range(NB):
            part = slice(b * size, (b + 1) * size)
            total += coeffs[index, b].astype(f32) * dot(vert[part], basis[part, :])
        return total.astype(bf16)

    def tile_copy(j, d):
        return pltpu.make_async_remote_copy(
            src_ref=send.at[j], dst_ref=recv.at[j],
            send_sem=send_sem.at[j], recv_sem=recv_sem.at[j],
            device_id={"skyx": lax.rem(me + d, n)}, device_id_type=MESH,
        )

    def distance(step):
        t = step // CAP
        odd = lax.rem(t, 2)
        return n // 2 + ((t + 1) // 2) * (2 * odd - 1)

    load_tiles.wait()
    load_basis.wait()
    load_coeffs.wait()

    def send_one(step, carry):
        d = distance(step)
        s = lax.rem(step, CAP)
        j = d * CAP + s
        send[j] = match(which(lax.rem(me + d, n) * CAP + s))
        tile_copy(j, d).start()
        return carry

    steps = CAP * (n - 1)
    lax.fori_loop(0, steps, send_one, 0)

    def own(s, carry):
        recv[s] = match(which(me * CAP + s))
        return carry

    lax.fori_loop(0, CAP, own, 0)

    numer[...] = jnp.zeros_like(numer)

    def weight_in(d, carry):
        copy = weight_copy(d)
        copy.wait_recv()
        copy.wait_send()
        return carry

    lax.fori_loop(1, n, weight_in, 0)

    pixel = lax.broadcasted_iota(jnp.int32, (1, patch), 1)

    def place(j, d):
        s = lax.rem(j, CAP)
        slot = lax.rem(me - d + n, n) * CAP + s
        oy, ox = offs[0, 0, slot], offs[1, 0, slot]
        w = wrecv[d, pl.ds(s, 1), :]
        w = jnp.concatenate([w] * (patch // LANES), axis=1)
        rowcov[pl.ds(j, 1), :] = jnp.where((pixel >= oy) & (pixel < oy + size), 1.0, 0.0)
        colcov[pl.ds(j, 1), :] = jnp.where((pixel >= ox) & (pixel < ox + size), w, 0.0)
        r = lax.broadcasted_iota(jnp.int32, (patch, size), 0) - lax.broadcasted_iota(jnp.int32, (patch, size), 1)
        rowhit = jnp.where(r == oy, 1.0, 0.0).astype(bf16)
        c = lax.broadcasted_iota(jnp.int32, (size, patch), 1) - lax.broadcasted_iota(jnp.int32, (size, patch), 0)
        colhit = jnp.where(c == ox, w, 0.0).astype(bf16)
        placed = dot(rowhit, recv[j]).astype(bf16)
        numer[...] += dot(placed, colhit)

    def place_own(s, carry):
        place(s, 0)
        return carry

    lax.fori_loop(0, CAP, place_own, 0)

    def place_one(step, carry):
        d = distance(step)
        j = d * CAP + lax.rem(step, CAP)
        tile_copy(j, d).wait_recv()
        place(j, d)
        return carry

    lax.fori_loop(0, steps, place_one, 0)

    load_bands.wait()
    cover = dot_0(rowcov[...].astype(bf16), colcov[...].astype(bf16))
    coadd = numer[...] / (1.0 + cover)
    numer[...] = coadd
    cb[...] = coadd.astype(bf16)
    hsend[...] = dot_t(pick[...], cb[...]).astype(bf16)

    def halo_copy(move):
        index, _, dy, dx, src, dst = move
        return pltpu.make_async_remote_copy(
            src_ref=src(), dst_ref=dst(),
            send_sem=hsend_sem.at[index], recv_sem=hrecv_sem.at[index],
            device_id={"skyy": row + dy, "skyx": me + dx}, device_id_type=MESH,
        )

    for move in moves:
        @pl.when(move[1])
        def _(move=move):
            halo_copy(move).start()

    store_coadd = pltpu.make_async_copy(numer, coadd_hbm, local_sem.at[2])
    store_coadd.start()

    vert = dot(gmid[...], cb[...])

    def drain(step, carry):
        d = distance(step)
        tile_copy(d * CAP + lax.rem(step, CAP), d).wait_send()
        return carry

    lax.fori_loop(0, steps, drain, 0)

    for move in moves:
        @pl.when(moves[opposite[move[0]]][1])
        def _(move=move):
            halo_copy(move).wait_recv()

    vert = (vert + dot_0(gedge[...], vhalo[...])).astype(bf16)
    sides = dot_t(gmid[...], hhalo[...]).astype(bf16)
    ends = dot_0(gedge[...], corner[...]).astype(bf16)
    result[...] = dot(vert, gmid[...]) + dot(sides, gedge[...]) + dot(ends, gcorner[...])
    store_result = pltpu.make_async_copy(result, detect_hbm, local_sem.at[3])
    store_result.start()
    for move in moves:
        @pl.when(move[1])
        def _(move=move):
            halo_copy(move).wait_send()
    store_coadd.wait()
    store_result.wait()


def body(rows, n, tiles, coeffs, weights, tile_slot, slot_offset):
    count, size = tiles.shape[1], tiles.shape[2]
    slots = n * CAP
    patch = PATCH
    f32, bf16 = jnp.float32, jnp.bfloat16
    basis = jnp.asarray(band_matrices(size))
    edge_at = np.concatenate([np.arange(-EDGE, 0), np.arange(patch, patch + EDGE)])
    corner_at = np.concatenate([np.arange(-LANES, 0), np.arange(patch, patch + LANES)])
    pick_at = np.concatenate([np.arange(EDGE), np.arange(patch - EDGE, patch)])
    pick = (pick_at[:, None] == np.arange(patch)[None, :]).astype(jnp.bfloat16)
    positions = np.concatenate([np.arange(patch), corner_at, edge_at])
    bands_np = np.concatenate([detect_matrix(positions, patch), pick])
    bands = jnp.asarray(bands_np)

    smem = pl.BlockSpec(memory_space=pltpu.SMEM)
    vmem = pl.BlockSpec(memory_space=pltpu.VMEM)
    anyspace = pl.BlockSpec(memory_space=pl.ANY)
    dma = pltpu.SemaphoreType.DMA
    return pl.pallas_call(
        functools.partial(kernel, rows, n),
        out_shape=[jax.ShapeDtypeStruct((patch, patch), f32)] * 2,
        in_specs=[smem] * 2 + [vmem] * 2 + [anyspace] * 4,
        out_specs=[anyspace] * 2,
        scratch_shapes=[
            pltpu.VMEM((count, size, size), bf16),
            pltpu.VMEM((count, NB, size, size), bf16),
            pltpu.VMEM((NB * size, size), bf16),
            pltpu.VMEM(bands_np.shape, bf16),
            pltpu.VMEM((slots, size, size), bf16),
            pltpu.VMEM((slots, size, size), bf16),
            pltpu.VMEM((n, 8, LANES), f32),
            pltpu.VMEM((n, 8, LANES), f32),
            pltpu.VMEM((patch, patch), f32),
            pltpu.VMEM((patch, patch), f32),
            pltpu.VMEM((slots, patch), f32),
            pltpu.VMEM((slots, patch), f32),
            pltpu.VMEM((patch, patch), bf16),
            pltpu.VMEM((2 * EDGE, patch), bf16),
            pltpu.VMEM((2 * EDGE, patch), bf16),
            pltpu.VMEM((2 * EDGE, patch), bf16),
            pltpu.VMEM((2 * EDGE, 2 * LANES), bf16),
            dma((6,)),
            dma((slots,)),
            dma((slots,)),
            dma((n,)),
            dma((n,)),
            dma((8,)),
            dma((8,)),
        ],
        compiler_params=pltpu.CompilerParams(
            collective_id=0, has_side_effects=True, vmem_limit_bytes=VMEM_LIMIT
        ),
        name="coadd",
    )(
        tile_slot, slot_offset, tile_slot, weights, tiles[0], coeffs[0], basis, bands,
    )


def solution(mesh):
    in_specs = (
        P("skyy", "skyx", None, None),
        P("skyy", "skyx", None, None, None),
        P("skyy", "skyx"),
        P("skyy", "skyx"),
        P(None, "skyy", "skyx"),
    )
    out_specs = (P("skyy", "skyx"), P("skyy", "skyx"))
    return jax.shard_map(
        functools.partial(body, mesh.shape["skyy"], mesh.shape["skyx"]),
        mesh=mesh, in_specs=in_specs, out_specs=out_specs, check_vma=False,
    )
```

```python
import functools

import jax
import jax.numpy as jnp
import numpy as np
from jax import lax
from jax.experimental import pallas as pl
from jax.experimental.pallas import tpu as pltpu
from jax.sharding import PartitionSpec as P

NB = 5
REACH = 10
CAP = 2
PATCH = 512
EDGE = 16
LANES = 128
VMEM_LIMIT = 63 * 1024 * 1024

basis_widths = (1.0, 1.8, 2.6, 3.6, 5.0)
detect_width = 2.5
MESH = pl.DeviceIdType.MESH


def band_matrices(size):
    rows = np.arange(size)[:, None]
    cols = np.arange(size)[None, :]
    gap = (cols - rows).astype(np.float32)
    inside = np.abs(cols - rows) <= REACH
    taps = np.arange(-REACH, REACH + 1).astype(np.float32)
    mats = []
    for width in basis_widths:
        total = np.sum(np.exp(-taps * taps / np.float32(2.0 * width * width)))
        mats.append(np.where(inside, np.exp(-gap * gap / np.float32(2.0 * width * width)) / total, 0.0))
    return np.concatenate(mats).astype(jnp.bfloat16)


def detect_matrix(positions, size):
    taps = np.arange(-REACH, REACH + 1).astype(np.float32)
    total = np.sum(np.exp(-taps * taps / np.float32(2.0 * detect_width * detect_width)))
    gap = np.asarray(positions)[:, None] - np.arange(size)[None, :]
    value = np.exp(-(gap * gap).astype(np.float32) / np.float32(2.0 * detect_width * detect_width)) / total
    return np.where(np.abs(gap) <= REACH, value, 0.0).astype(jnp.bfloat16)


def dot(a, b):
    return jnp.dot(a, b, preferred_element_type=jnp.float32)


def dot_t(a, b):
    return lax.dot_general(a, b, (((1,), (1,)), ((), ())), preferred_element_type=jnp.float32)


def dot_0(a, b):
    return lax.dot_general(a, b, (((0,), (0,)), ((), ())), preferred_element_type=jnp.float32)


def kernel(
    rows, n,
    slot_at, offs, slot_row, weight_row,
    tiles_hbm, coeffs_hbm, basis_hbm, bands_hbm,
    coadd_hbm, detect_hbm,
    tiles, coeffs, basis, bands, send_far, recv_far, send_near, recv_near, wsend, wrecv,
    osend, orecv, numer, inverse, result, part_out, part_in, rowcov, colcov,
    cb, vhalo, hsend, hhalo, corner, local_sem,
    far_send_sem, far_recv_sem, near_send_sem, near_recv_sem, wsend_sem, wrecv_sem,
    osend_sem, orecv_sem, part_send_sem, part_recv_sem, hsend_sem, hrecv_sem,
):
    row, me = lax.axis_index("skyy"), lax.axis_index("skyx")
    size = tiles.shape[1]
    patch = numer.shape[0]
    f32, bf16 = jnp.float32, jnp.bfloat16

    load_tiles = pltpu.make_async_copy(tiles_hbm, tiles, local_sem.at[0])
    load_coeffs = pltpu.make_async_copy(coeffs_hbm, coeffs, local_sem.at[1])
    load_basis = pltpu.make_async_copy(basis_hbm, basis, local_sem.at[4])
    load_bands = pltpu.make_async_copy(bands_hbm, bands, local_sem.at[5])
    load_tiles.start()
    load_basis.start()
    load_coeffs.start()
    load_bands.start()
    gmid = bands.at[pl.ds(0, patch), :]
    gcorner = bands.at[pl.ds(patch, 2 * LANES), :]
    gedge = bands.at[pl.ds(patch + 2 * LANES, 2 * EDGE), :]
    pick = bands.at[pl.ds(patch + 2 * LANES + 2 * EDGE, 2 * EDGE), :]

    vhalo[...] = jnp.zeros_like(vhalo)
    hhalo[...] = jnp.zeros_like(hhalo)
    corner[...] = jnp.zeros_like(corner)

    up, down, left, right = row > 0, row < rows - 1, me > 0, me < n - 1
    both = jnp.logical_and
    span, width = n // 2, n // 4
    half = me // span
    local = me - half * span
    column = lax.rem(me, width)
    inner = me // width == 1 + half
    moves = [
        (0, up, -1, 0, lambda: cb.at[pl.ds(0, EDGE), :], lambda: vhalo.at[pl.ds(EDGE, EDGE), :]),
        (1, down, 1, 0, lambda: cb.at[pl.ds(patch - EDGE, EDGE), :], lambda: vhalo.at[pl.ds(0, EDGE), :]),
        (2, left, 0, -1, lambda: hsend.at[pl.ds(0, EDGE), :], lambda: hhalo.at[pl.ds(EDGE, EDGE), :]),
        (3, right, 0, 1, lambda: hsend.at[pl.ds(EDGE, EDGE), :], lambda: hhalo.at[pl.ds(0, EDGE), :]),
        (4, both(up, left), -1, -1, lambda: cb.at[pl.ds(0, EDGE), pl.ds(0, LANES)],
         lambda: corner.at[pl.ds(EDGE, EDGE), pl.ds(LANES, LANES)]),
        (5, both(up, right), -1, 1, lambda: cb.at[pl.ds(0, EDGE), pl.ds(patch - LANES, LANES)],
         lambda: corner.at[pl.ds(EDGE, EDGE), pl.ds(0, LANES)]),
        (6, both(down, left), 1, -1, lambda: cb.at[pl.ds(patch - EDGE, EDGE), pl.ds(0, LANES)],
         lambda: corner.at[pl.ds(0, EDGE), pl.ds(LANES, LANES)]),
        (7, both(down, right), 1, 1, lambda: cb.at[pl.ds(patch - EDGE, EDGE), pl.ds(patch - LANES, LANES)],
         lambda: corner.at[pl.ds(0, EDGE), pl.ds(0, LANES)]),
    ]
    opposite = {0: 1, 1: 0, 2: 3, 3: 2, 4: 7, 5: 6, 6: 5, 7: 4}

    barrier = pltpu.get_barrier_semaphore()

    def greet(d, carry):
        pl.semaphore_signal(barrier, inc=1, device_id={"skyx": lax.rem(me + d, n)}, device_id_type=MESH)
        return carry

    lax.fori_loop(1, n, greet, 0)
    expected = n - 1
    for index, exists, dy, dx, _, _ in moves:
        if dy != 0:
            @pl.when(exists)
            def _(dy=dy, dx=dx):
                pl.semaphore_signal(
                    barrier, inc=1, device_id={"skyy": row + dy, "skyx": me + dx}, device_id_type=MESH
                )
            expected = expected + jnp.where(exists, 1, 0)
    pl.semaphore_wait(barrier, expected)

    def weight_copy(d):
        return pltpu.make_async_remote_copy(
            src_ref=wsend.at[d], dst_ref=wrecv.at[d],
            send_sem=wsend_sem.at[d], recv_sem=wrecv_sem.at[d],
            device_id={"skyx": lax.rem(me + d, n)}, device_id_type=MESH,
        )

    line = lax.broadcasted_iota(jnp.int32, (8, LANES), 0)

    weight_of = weight_row[...].astype(f32)
    count = tiles.shape[0]

    def slot_weight(slot):
        return jnp.sum(jnp.where(slot_row[...] == slot, weight_of, 0.0), axis=1, keepdims=True)

    def far_patch(side, p, at):
        return ((3 - p) - side * (3 - 2 * p)) * width + at

    def weight_block(dest):
        side, at = dest // span, lax.rem(dest, width)
        block = jnp.zeros((8, LANES), f32)
        for p, patch_at in enumerate((dest, far_patch(side, 0, at), far_patch(side, 1, at))):
            for s in range(CAP):
                block = jnp.where(line == p * CAP + s, slot_weight(patch_at * CAP + s), block)
        return block

    def write_offset(j, carry):
        osend[pl.ds(2 * j, 1), :] = jnp.full((1, LANES), offs[0, 0, j], jnp.int32)
        osend[pl.ds(2 * j + 1, 1), :] = jnp.full((1, LANES), offs[1, 0, j], jnp.int32)
        return carry

    def offset_copy(p):
        return pltpu.make_async_remote_copy(
            src_ref=osend, dst_ref=orecv.at[p],
            send_sem=osend_sem.at[0], recv_sem=orecv_sem.at[p],
            device_id={"skyx": (2 - half) * width + column}, device_id_type=MESH,
        )

    my_kind = jnp.where(inner, 1, 0)
    lax.fori_loop(0, n * CAP, write_offset, 0)
    offset_copy(my_kind).start()

    def which(slot):
        index = jnp.int32(0)
        for m in range(count):
            index = jnp.where(slot_at[0, m] == slot, m, index)
        return index

    def send_weight(d, carry):
        wsend[d] = weight_block(lax.rem(me + d, n))
        weight_copy(d).start()
        return carry

    wrecv[0] = weight_block(me)
    lax.fori_loop(1, n, send_weight, 0)

    def match(index):
        x = tiles[index]
        vert = dot(basis[...], x).astype(bf16)
        total = jnp.zeros((size, size), f32)
        for b in range(NB):
            part = slice(b * size, (b + 1) * size)
            total += coeffs[index, b].astype(f32) * dot(vert[part], basis[part, :])
        return total.astype(bf16)

    def far_slot(p, sender, s):
        return (p * span + sender) * CAP + s

    def far_copy(p, at, s, sender):
        out = (p * width + at) * CAP + s
        slot = far_slot(p, sender, s)
        return pltpu.make_async_remote_copy(
            src_ref=send_far.at[out], dst_ref=recv_far.at[slot],
            send_sem=far_send_sem.at[out], recv_sem=far_recv_sem.at[slot],
            device_id={"skyx": (1 + half) * width + at}, device_id_type=MESH,
        )

    def near_copy(dest, s, sender):
        return pltpu.make_async_remote_copy(
            src_ref=send_near.at[dest * CAP + s], dst_ref=recv_near.at[sender * CAP + s],
            send_sem=near_send_sem.at[dest * CAP + s], recv_sem=near_recv_sem.at[sender * CAP + s],
            device_id={"skyx": half * span + dest}, device_id_type=MESH,
        )

    def part_copy(p):
        return pltpu.make_async_remote_copy(
            src_ref=part_out.at[p], dst_ref=part_in,
            send_sem=part_send_sem.at[p], recv_sem=part_recv_sem.at[0],
            device_id={"skyx": far_patch(half, p, column)}, device_id_type=MESH,
        )

    def far_step(step):
        p = step // (width * CAP)
        at = lax.rem(column + lax.rem(step // CAP, width), width)
        mine = both(inner, at == column)
        return p, at, lax.rem(step, CAP), mine

    def near_step(step):
        t = step // CAP
        d = span // 2 + ((t + 1) // 2) * (2 * lax.rem(t, 2) - 1)
        return d, lax.rem(step, CAP)

    far_steps, near_steps = 2 * width * CAP, CAP * (span - 1)

    load_tiles.wait()
    load_basis.wait()
    load_coeffs.wait()

    def send_one_far(step, carry):
        p, at, s, mine = far_step(step)
        tile = match(which(far_patch(half, p, at) * CAP + s))

        @pl.when(mine)
        def _():
            recv_far[far_slot(p, local, s)] = tile

        @pl.when(jnp.logical_not(mine))
        def _():
            send_far[(p * width + at) * CAP + s] = tile
            far_copy(p, at, s, local).start()

        return carry

    lax.fori_loop(0, far_steps, send_one_far, 0)

    def send_one_near(step, carry):
        d, s = near_step(step)
        dest = lax.rem(local + d, span)
        send_near[dest * CAP + s] = match(which((half * span + dest) * CAP + s))
        near_copy(dest, s, local).start()
        return carry

    lax.fori_loop(0, near_steps, send_one_near, 0)

    def own(s, carry):
        recv_near[local * CAP + s] = match(which(me * CAP + s))
        return carry

    lax.fori_loop(0, CAP, own, 0)

    numer[...] = jnp.zeros_like(numer)

    def weight_in(d, carry):
        copy = weight_copy(d)
        copy.wait_recv()
        copy.wait_send()
        return carry

    lax.fori_loop(1, n, weight_in, 0)

    pixel = lax.broadcasted_iota(jnp.int32, (1, patch), 1)

    def wide(line_of, size):
        return jnp.concatenate([line_of] * (size // LANES), axis=1)

    def weight_at(sender, kind, s):
        return wrecv[lax.rem(me - sender + n, n), pl.ds(kind * CAP + s, 1), :]

    def cover_one(j, carry):
        oy, ox = offs[0, 0, j], offs[1, 0, j]
        w = wide(weight_at(j // CAP, 0, lax.rem(j, CAP)), patch)
        rowcov[pl.ds(j, 1), :] = jnp.where((pixel >= oy) & (pixel < oy + size), 1.0, 0.0)
        colcov[pl.ds(j, 1), :] = jnp.where((pixel >= ox) & (pixel < ox + size), w, 0.0)
        return carry

    lax.fori_loop(0, n * CAP, cover_one, 0)
    cover = dot_0(rowcov[...].astype(bf16), colcov[...].astype(bf16))
    inverse[...] = 1.0 / (1.0 + cover)

    def place(total, tile, oy, ox, w):
        r = lax.broadcasted_iota(jnp.int32, (patch, size), 0) - lax.broadcasted_iota(jnp.int32, (patch, size), 1)
        rowhit = jnp.where(r == wide(oy, size), 1.0, 0.0).astype(bf16)
        c = lax.broadcasted_iota(jnp.int32, (size, patch), 1) - lax.broadcasted_iota(jnp.int32, (size, patch), 0)
        colhit = jnp.where(c == wide(ox, patch), wide(w, patch), 0.0).astype(bf16)
        placed = dot(rowhit, tile).astype(bf16)
        total[...] += dot(placed, colhit)

    @pl.when(inner)
    def _():
        offset_copy(0).wait_recv()
        offset_copy(1).wait_recv()

        def sum_far(p, carry):
            result[...] = jnp.zeros_like(result)

            def add_far(step, carry):
                sender = lax.rem(local + step // CAP, span)
                s = lax.rem(step, CAP)

                @pl.when(sender != local)
                def _():
                    far_copy(p, column, s, sender).wait_recv()

                whole = half * span + sender
                at = 2 * (whole * CAP + s)
                place(
                    result, recv_far[far_slot(p, sender, s)],
                    orecv[p, pl.ds(at, 1), :], orecv[p, pl.ds(at + 1, 1), :],
                    weight_at(whole, 1 + p, s),
                )
                return carry

            lax.fori_loop(0, span * CAP, add_far, 0)
            part_out[p] = result[...].astype(bf16)
            part_copy(p).start()
            return carry

        lax.fori_loop(0, 2, sum_far, 0)

    def add_near(step, carry):
        sender = lax.rem(local + step // CAP, span)
        s = lax.rem(step, CAP)

        @pl.when(sender != local)
        def _():
            near_copy(local, s, sender).wait_recv()

        whole = half * span + sender
        at = 2 * (whole * CAP + s)
        place(
            numer, recv_near[sender * CAP + s],
            osend[pl.ds(at, 1), :], osend[pl.ds(at + 1, 1), :], weight_at(whole, 0, s),
        )
        return carry

    lax.fori_loop(0, span * CAP, add_near, 0)
    part_copy(0).wait_recv()
    load_bands.wait()
    coadd = (numer[...] + part_in[...].astype(f32)) * inverse[...]
    numer[...] = coadd
    cb[...] = coadd.astype(bf16)
    hsend[...] = dot_t(pick[...], cb[...]).astype(bf16)

    def halo_copy(move):
        index, _, dy, dx, src, dst = move
        return pltpu.make_async_remote_copy(
            src_ref=src(), dst_ref=dst(),
            send_sem=hsend_sem.at[index], recv_sem=hrecv_sem.at[index],
            device_id={"skyy": row + dy, "skyx": me + dx}, device_id_type=MESH,
        )

    for move in moves:
        @pl.when(move[1])
        def _(move=move):
            halo_copy(move).start()

    store_coadd = pltpu.make_async_copy(numer, coadd_hbm, local_sem.at[2])
    store_coadd.start()

    vert = dot(gmid[...], cb[...])

    def drain_far(step, carry):
        p, at, s, mine = far_step(step)

        @pl.when(jnp.logical_not(mine))
        def _():
            far_copy(p, at, s, local).wait_send()

        return carry

    def drain_near(step, carry):
        d, s = near_step(step)
        near_copy(lax.rem(local + d, span), s, local).wait_send()
        return carry

    lax.fori_loop(0, far_steps, drain_far, 0)
    lax.fori_loop(0, near_steps, drain_near, 0)
    offset_copy(my_kind).wait_send()

    @pl.when(inner)
    def _():
        part_copy(0).wait_send()
        part_copy(1).wait_send()

    for move in moves:
        @pl.when(moves[opposite[move[0]]][1])
        def _(move=move):
            halo_copy(move).wait_recv()

    vert = (vert + dot_0(gedge[...], vhalo[...])).astype(bf16)
    sides = dot_t(gmid[...], hhalo[...]).astype(bf16)
    ends = dot_0(gedge[...], corner[...]).astype(bf16)
    result[...] = dot(vert, gmid[...]) + dot(sides, gedge[...]) + dot(ends, gcorner[...])
    store_result = pltpu.make_async_copy(result, detect_hbm, local_sem.at[3])
    store_result.start()
    for move in moves:
        @pl.when(move[1])
        def _(move=move):
            halo_copy(move).wait_send()
    store_coadd.wait()
    store_result.wait()


def body(rows, n, tiles, coeffs, weights, tile_slot, slot_offset):
    count, size = tiles.shape[1], tiles.shape[2]
    slots = n * CAP
    patch = PATCH
    f32, bf16 = jnp.float32, jnp.bfloat16
    basis = jnp.asarray(band_matrices(size))
    edge_at = np.concatenate([np.arange(-EDGE, 0), np.arange(patch, patch + EDGE)])
    corner_at = np.concatenate([np.arange(-LANES, 0), np.arange(patch, patch + LANES)])
    pick_at = np.concatenate([np.arange(EDGE), np.arange(patch - EDGE, patch)])
    pick = (pick_at[:, None] == np.arange(patch)[None, :]).astype(jnp.bfloat16)
    positions = np.concatenate([np.arange(patch), corner_at, edge_at])
    bands_np = np.concatenate([detect_matrix(positions, patch), pick])
    bands = jnp.asarray(bands_np)

    smem = pl.BlockSpec(memory_space=pltpu.SMEM)
    vmem = pl.BlockSpec(memory_space=pltpu.VMEM)
    anyspace = pl.BlockSpec(memory_space=pl.ANY)
    dma = pltpu.SemaphoreType.DMA
    return pl.pallas_call(
        functools.partial(kernel, rows, n),
        out_shape=[jax.ShapeDtypeStruct((patch, patch), f32)] * 2,
        in_specs=[smem] * 2 + [vmem] * 2 + [anyspace] * 4,
        out_specs=[anyspace] * 2,
        scratch_shapes=[
            pltpu.VMEM((count, size, size), bf16),
            pltpu.VMEM((count, NB, size, size), bf16),
            pltpu.VMEM((NB * size, size), bf16),
            pltpu.VMEM(bands_np.shape, bf16),
            pltpu.VMEM((slots // 2, size, size), bf16),
            pltpu.VMEM((slots, size, size), bf16),
            pltpu.VMEM((slots // 2, size, size), bf16),
            pltpu.VMEM((slots // 2, size, size), bf16),
            pltpu.VMEM((n, 8, LANES), f32),
            pltpu.VMEM((n, 8, LANES), f32),
            pltpu.VMEM((2 * slots, LANES), jnp.int32),
            pltpu.VMEM((2, 2 * slots, LANES), jnp.int32),
            pltpu.VMEM((patch, patch), f32),
            pltpu.VMEM((patch, patch), f32),
            pltpu.VMEM((patch, patch), f32),
            pltpu.VMEM((2, patch, patch), bf16),
            pltpu.VMEM((patch, patch), bf16),
            pltpu.VMEM((slots, patch), f32),
            pltpu.VMEM((slots, patch), f32),
            pltpu.VMEM((patch, patch), bf16),
            pltpu.VMEM((2 * EDGE, patch), bf16),
            pltpu.VMEM((2 * EDGE, patch), bf16),
            pltpu.VMEM((2 * EDGE, patch), bf16),
            pltpu.VMEM((2 * EDGE, 2 * LANES), bf16),
            dma((6,)),
            dma((slots // 2,)),
            dma((slots,)),
            dma((slots // 2,)),
            dma((slots // 2,)),
            dma((n,)),
            dma((n,)),
            dma((1,)),
            dma((2,)),
            dma((2,)),
            dma((1,)),
            dma((8,)),
            dma((8,)),
        ],
        compiler_params=pltpu.CompilerParams(
            collective_id=0, has_side_effects=True, vmem_limit_bytes=VMEM_LIMIT
        ),
        name="coadd",
    )(
        tile_slot, slot_offset, tile_slot, weights, tiles[0], coeffs[0], basis, bands,
    )


def solution(mesh):
    in_specs = (
        P("skyy", "skyx", None, None),
        P("skyy", "skyx", None, None, None),
        P("skyy", "skyx"),
        P("skyy", "skyx"),
        P(None, "skyy", "skyx"),
    )
    out_specs = (P("skyy", "skyx"), P("skyy", "skyx"))
    return jax.shard_map(
        functools.partial(body, mesh.shape["skyy"], mesh.shape["skyx"]),
        mesh=mesh, in_specs=in_specs, out_specs=out_specs, check_vma=False,
    )
```

```python
import functools

import jax
import jax.numpy as jnp
import numpy as np
from jax import lax
from jax.experimental import pallas as pl
from jax.experimental.pallas import tpu as pltpu
from jax.sharding import PartitionSpec as P

NB = 5
REACH = 10
CAP = 2
PATCH = 512
EDGE = 16
LANES = 128
VMEM_LIMIT = 63 * 1024 * 1024

basis_widths = (1.0, 1.8, 2.6, 3.6, 5.0)
detect_width = 2.5
MESH = pl.DeviceIdType.MESH


def band_matrices(size):
    rows = np.arange(size)[:, None]
    cols = np.arange(size)[None, :]
    gap = (cols - rows).astype(np.float32)
    inside = np.abs(cols - rows) <= REACH
    taps = np.arange(-REACH, REACH + 1).astype(np.float32)
    mats = []
    for width in basis_widths:
        total = np.sum(np.exp(-taps * taps / np.float32(2.0 * width * width)))
        mats.append(np.where(inside, np.exp(-gap * gap / np.float32(2.0 * width * width)) / total, 0.0))
    return np.concatenate(mats).astype(jnp.bfloat16)


def detect_matrix(positions, size):
    taps = np.arange(-REACH, REACH + 1).astype(np.float32)
    total = np.sum(np.exp(-taps * taps / np.float32(2.0 * detect_width * detect_width)))
    gap = np.asarray(positions)[:, None] - np.arange(size)[None, :]
    value = np.exp(-(gap * gap).astype(np.float32) / np.float32(2.0 * detect_width * detect_width)) / total
    return np.where(np.abs(gap) <= REACH, value, 0.0).astype(jnp.bfloat16)


def dot(a, b):
    return jnp.dot(a, b, preferred_element_type=jnp.float32)


def dot_t(a, b):
    return lax.dot_general(a, b, (((1,), (1,)), ((), ())), preferred_element_type=jnp.float32)


def dot_0(a, b):
    return lax.dot_general(a, b, (((0,), (0,)), ((), ())), preferred_element_type=jnp.float32)


def kernel(
    rows, n,
    slot_at, offs, slot_row, weight_row,
    tiles_hbm, coeffs_hbm, basis_hbm, bands_hbm,
    coadd_hbm, vert_hbm, sides_hbm, ends_hbm,
    tiles, coeffs, basis, bands, send_far, recv_far, send_near, recv_near, wsend, wrecv,
    osend, orecv, numer, inverse, result, part_out, part_in, rowcov, colcov,
    cb, vhalo, hsend, hhalo, corner, vert_out, sides_out, ends_out, local_sem,
    far_send_sem, far_recv_sem, near_send_sem, near_recv_sem, wsend_sem, wrecv_sem,
    osend_sem, orecv_sem, part_send_sem, part_recv_sem, hsend_sem, hrecv_sem,
):
    row, me = lax.axis_index("skyy"), lax.axis_index("skyx")
    size = tiles.shape[1]
    patch = numer.shape[0]
    f32, bf16 = jnp.float32, jnp.bfloat16

    load_tiles = pltpu.make_async_copy(tiles_hbm, tiles, local_sem.at[0])
    load_coeffs = pltpu.make_async_copy(coeffs_hbm, coeffs, local_sem.at[1])
    load_basis = pltpu.make_async_copy(basis_hbm, basis, local_sem.at[4])
    load_bands = pltpu.make_async_copy(bands_hbm, bands, local_sem.at[5])
    load_tiles.start()
    load_basis.start()
    load_coeffs.start()
    load_bands.start()
    gmid = bands.at[pl.ds(0, patch), :]
    gedge = bands.at[pl.ds(patch + 2 * LANES, 2 * EDGE), :]
    pick = bands.at[pl.ds(patch + 2 * LANES + 2 * EDGE, 2 * EDGE), :]

    vhalo[...] = jnp.zeros_like(vhalo)
    hhalo[...] = jnp.zeros_like(hhalo)
    corner[...] = jnp.zeros_like(corner)

    up, down, left, right = row > 0, row < rows - 1, me > 0, me < n - 1
    both = jnp.logical_and
    span, width = n // 2, n // 4
    half = me // span
    local = me - half * span
    column = lax.rem(me, width)
    inner = me // width == 1 + half
    moves = [
        (0, up, -1, 0, lambda: cb.at[pl.ds(0, EDGE), :], lambda: vhalo.at[pl.ds(EDGE, EDGE), :]),
        (1, down, 1, 0, lambda: cb.at[pl.ds(patch - EDGE, EDGE), :], lambda: vhalo.at[pl.ds(0, EDGE), :]),
        (2, left, 0, -1, lambda: hsend.at[pl.ds(0, EDGE), :], lambda: hhalo.at[pl.ds(EDGE, EDGE), :]),
        (3, right, 0, 1, lambda: hsend.at[pl.ds(EDGE, EDGE), :], lambda: hhalo.at[pl.ds(0, EDGE), :]),
        (4, both(up, left), -1, -1, lambda: cb.at[pl.ds(0, EDGE), pl.ds(0, LANES)],
         lambda: corner.at[pl.ds(EDGE, EDGE), pl.ds(LANES, LANES)]),
        (5, both(up, right), -1, 1, lambda: cb.at[pl.ds(0, EDGE), pl.ds(patch - LANES, LANES)],
         lambda: corner.at[pl.ds(EDGE, EDGE), pl.ds(0, LANES)]),
        (6, both(down, left), 1, -1, lambda: cb.at[pl.ds(patch - EDGE, EDGE), pl.ds(0, LANES)],
         lambda: corner.at[pl.ds(0, EDGE), pl.ds(LANES, LANES)]),
        (7, both(down, right), 1, 1, lambda: cb.at[pl.ds(patch - EDGE, EDGE), pl.ds(patch - LANES, LANES)],
         lambda: corner.at[pl.ds(0, EDGE), pl.ds(0, LANES)]),
    ]
    opposite = {0: 1, 1: 0, 2: 3, 3: 2, 4: 7, 5: 6, 6: 5, 7: 4}

    barrier = pltpu.get_barrier_semaphore()

    def greet(d, carry):
        pl.semaphore_signal(barrier, inc=1, device_id={"skyx": lax.rem(me + d, n)}, device_id_type=MESH)
        return carry

    lax.fori_loop(1, n, greet, 0)
    expected = n - 1
    for index, exists, dy, dx, _, _ in moves:
        if dy != 0:
            @pl.when(exists)
            def _(dy=dy, dx=dx):
                pl.semaphore_signal(
                    barrier, inc=1, device_id={"skyy": row + dy, "skyx": me + dx}, device_id_type=MESH
                )
            expected = expected + jnp.where(exists, 1, 0)
    pl.semaphore_wait(barrier, expected)

    def weight_copy(d):
        return pltpu.make_async_remote_copy(
            src_ref=wsend.at[d], dst_ref=wrecv.at[d],
            send_sem=wsend_sem.at[d], recv_sem=wrecv_sem.at[d],
            device_id={"skyx": lax.rem(me + d, n)}, device_id_type=MESH,
        )

    line = lax.broadcasted_iota(jnp.int32, (8, LANES), 0)

    weight_of = weight_row[...].astype(f32)
    count = tiles.shape[0]

    def slot_weight(slot):
        return jnp.sum(jnp.where(slot_row[...] == slot, weight_of, 0.0), axis=1, keepdims=True)

    def far_patch(side, p, at):
        return ((3 - p) - side * (3 - 2 * p)) * width + at

    def weight_block(dest):
        side, at = dest // span, lax.rem(dest, width)
        block = jnp.zeros((8, LANES), f32)
        for p, patch_at in enumerate((dest, far_patch(side, 0, at), far_patch(side, 1, at))):
            for s in range(CAP):
                block = jnp.where(line == p * CAP + s, slot_weight(patch_at * CAP + s), block)
        return block

    def write_offset(j, carry):
        osend[pl.ds(2 * j, 1), :] = jnp.full((1, LANES), offs[0, 0, j], jnp.int32)
        osend[pl.ds(2 * j + 1, 1), :] = jnp.full((1, LANES), offs[1, 0, j], jnp.int32)
        return carry

    def offset_copy(p):
        return pltpu.make_async_remote_copy(
            src_ref=osend, dst_ref=orecv.at[p],
            send_sem=osend_sem.at[0], recv_sem=orecv_sem.at[p],
            device_id={"skyx": (2 - half) * width + column}, device_id_type=MESH,
        )

    my_kind = jnp.where(inner, 1, 0)
    lax.fori_loop(0, n * CAP, write_offset, 0)
    offset_copy(my_kind).start()

    def which(slot):
        index = jnp.int32(0)
        for m in range(count):
            index = jnp.where(slot_at[0, m] == slot, m, index)
        return index

    def send_weight(d, carry):
        wsend[d] = weight_block(lax.rem(me + d, n))
        weight_copy(d).start()
        return carry

    wrecv[0] = weight_block(me)
    lax.fori_loop(1, n, send_weight, 0)

    def match(index):
        x = tiles[index]
        vert = dot(basis[...], x).astype(bf16)
        total = jnp.zeros((size, size), f32)
        for b in range(NB):
            part = slice(b * size, (b + 1) * size)
            total += coeffs[index, b].astype(f32) * dot(vert[part], basis[part, :])
        return total.astype(bf16)

    def far_slot(p, sender, s):
        return (p * span + sender) * CAP + s

    def far_copy(p, at, s, sender):
        out = (p * width + at) * CAP + s
        slot = far_slot(p, sender, s)
        return pltpu.make_async_remote_copy(
            src_ref=send_far.at[out], dst_ref=recv_far.at[slot],
            send_sem=far_send_sem.at[out], recv_sem=far_recv_sem.at[slot],
            device_id={"skyx": (1 + half) * width + at}, device_id_type=MESH,
        )

    def near_copy(dest, s, sender):
        return pltpu.make_async_remote_copy(
            src_ref=send_near.at[dest * CAP + s], dst_ref=recv_near.at[sender * CAP + s],
            send_sem=near_send_sem.at[dest * CAP + s], recv_sem=near_recv_sem.at[sender * CAP + s],
            device_id={"skyx": half * span + dest}, device_id_type=MESH,
        )

    def part_copy(p):
        return pltpu.make_async_remote_copy(
            src_ref=part_out.at[p], dst_ref=part_in,
            send_sem=part_send_sem.at[p], recv_sem=part_recv_sem.at[0],
            device_id={"skyx": far_patch(half, p, column)}, device_id_type=MESH,
        )

    def far_step(step):
        p = step // (width * CAP)
        at = lax.rem(column + lax.rem(step // CAP, width), width)
        mine = both(inner, at == column)
        return p, at, lax.rem(step, CAP), mine

    def near_step(step):
        t = step // CAP
        d = span // 2 + ((t + 1) // 2) * (2 * lax.rem(t, 2) - 1)
        return d, lax.rem(step, CAP)

    far_steps, near_steps = 2 * width * CAP, CAP * (span - 1)

    load_tiles.wait()
    load_basis.wait()
    load_coeffs.wait()

    def send_one_far(step, carry):
        p, at, s, mine = far_step(step)
        tile = match(which(far_patch(half, p, at) * CAP + s))

        @pl.when(mine)
        def _():
            recv_far[far_slot(p, local, s)] = tile

        @pl.when(jnp.logical_not(mine))
        def _():
            send_far[(p * width + at) * CAP + s] = tile
            far_copy(p, at, s, local).start()

        return carry

    lax.fori_loop(0, far_steps, send_one_far, 0)

    def send_one_near(step, carry):
        d, s = near_step(step)
        dest = lax.rem(local + d, span)
        send_near[dest * CAP + s] = match(which((half * span + dest) * CAP + s))
        near_copy(dest, s, local).start()
        return carry

    lax.fori_loop(0, near_steps, send_one_near, 0)

    def own(s, carry):
        recv_near[local * CAP + s] = match(which(me * CAP + s))
        return carry

    lax.fori_loop(0, CAP, own, 0)

    numer[...] = jnp.zeros_like(numer)

    def weight_in(d, carry):
        copy = weight_copy(d)
        copy.wait_recv()
        copy.wait_send()
        return carry

    lax.fori_loop(1, n, weight_in, 0)

    pixel = lax.broadcasted_iota(jnp.int32, (1, patch), 1)

    def wide(line_of, size):
        return jnp.concatenate([line_of] * (size // LANES), axis=1)

    def weight_at(sender, kind, s):
        return wrecv[lax.rem(me - sender + n, n), pl.ds(kind * CAP + s, 1), :]

    def cover_one(j, carry):
        oy, ox = offs[0, 0, j], offs[1, 0, j]
        w = wide(weight_at(j // CAP, 0, lax.rem(j, CAP)), patch)
        rowcov[pl.ds(j, 1), :] = jnp.where((pixel >= oy) & (pixel < oy + size), 1.0, 0.0)
        colcov[pl.ds(j, 1), :] = jnp.where((pixel >= ox) & (pixel < ox + size), w, 0.0)
        return carry

    lax.fori_loop(0, n * CAP, cover_one, 0)
    cover = dot_0(rowcov[...].astype(bf16), colcov[...].astype(bf16))
    inverse[...] = 1.0 / (1.0 + cover)

    def place(total, tile, oy, ox, w):
        r = lax.broadcasted_iota(jnp.int32, (patch, size), 0) - lax.broadcasted_iota(jnp.int32, (patch, size), 1)
        rowhit = jnp.where(r == wide(oy, size), 1.0, 0.0).astype(bf16)
        c = lax.broadcasted_iota(jnp.int32, (size, patch), 1) - lax.broadcasted_iota(jnp.int32, (size, patch), 0)
        colhit = jnp.where(c == wide(ox, patch), wide(w, patch), 0.0).astype(bf16)
        placed = dot(rowhit, tile).astype(bf16)
        total[...] += dot(placed, colhit)

    @pl.when(inner)
    def _():
        offset_copy(0).wait_recv()
        offset_copy(1).wait_recv()

        def sum_far(p, carry):
            result[...] = jnp.zeros_like(result)

            def add_far(step, carry):
                sender = lax.rem(local + step // CAP, span)
                s = lax.rem(step, CAP)

                @pl.when(sender != local)
                def _():
                    far_copy(p, column, s, sender).wait_recv()

                whole = half * span + sender
                at = 2 * (whole * CAP + s)
                place(
                    result, recv_far[far_slot(p, sender, s)],
                    orecv[p, pl.ds(at, 1), :], orecv[p, pl.ds(at + 1, 1), :],
                    weight_at(whole, 1 + p, s),
                )
                return carry

            lax.fori_loop(0, span * CAP, add_far, 0)
            part_out[p] = result[...].astype(bf16)
            part_copy(p).start()
            return carry

        lax.fori_loop(0, 2, sum_far, 0)

    def add_near(step, carry):
        sender = lax.rem(local + step // CAP, span)
        s = lax.rem(step, CAP)

        @pl.when(sender != local)
        def _():
            near_copy(local, s, sender).wait_recv()

        whole = half * span + sender
        at = 2 * (whole * CAP + s)
        place(
            numer, recv_near[sender * CAP + s],
            osend[pl.ds(at, 1), :], osend[pl.ds(at + 1, 1), :], weight_at(whole, 0, s),
        )
        return carry

    lax.fori_loop(0, span * CAP, add_near, 0)
    part_copy(0).wait_recv()
    load_bands.wait()
    coadd = (numer[...] + part_in[...].astype(f32)) * inverse[...]
    numer[...] = coadd
    cb[...] = coadd.astype(bf16)
    hsend[...] = dot_t(pick[...], cb[...]).astype(bf16)

    def halo_copy(move):
        index, _, dy, dx, src, dst = move
        return pltpu.make_async_remote_copy(
            src_ref=src(), dst_ref=dst(),
            send_sem=hsend_sem.at[index], recv_sem=hrecv_sem.at[index],
            device_id={"skyy": row + dy, "skyx": me + dx}, device_id_type=MESH,
        )

    for move in moves:
        @pl.when(move[1])
        def _(move=move):
            halo_copy(move).start()

    store_coadd = pltpu.make_async_copy(numer, coadd_hbm, local_sem.at[2])
    store_coadd.start()

    vert = dot(gmid[...], cb[...])

    def drain_far(step, carry):
        p, at, s, mine = far_step(step)

        @pl.when(jnp.logical_not(mine))
        def _():
            far_copy(p, at, s, local).wait_send()

        return carry

    def drain_near(step, carry):
        d, s = near_step(step)
        near_copy(lax.rem(local + d, span), s, local).wait_send()
        return carry

    lax.fori_loop(0, far_steps, drain_far, 0)
    lax.fori_loop(0, near_steps, drain_near, 0)
    offset_copy(my_kind).wait_send()

    @pl.when(inner)
    def _():
        part_copy(0).wait_send()
        part_copy(1).wait_send()

    for move in moves:
        @pl.when(moves[opposite[move[0]]][1])
        def _(move=move):
            halo_copy(move).wait_recv()

    vert_out[...] = (vert + dot_0(gedge[...], vhalo[...])).astype(bf16)
    sides_out[...] = dot_t(gmid[...], hhalo[...]).astype(bf16)
    ends_out[...] = dot_0(gedge[...], corner[...]).astype(bf16)
    stores = [
        pltpu.make_async_copy(src, dst, local_sem.at[at])
        for src, dst, at in ((vert_out, vert_hbm, 3), (sides_out, sides_hbm, 6), (ends_out, ends_hbm, 7))
    ]
    for store in stores:
        store.start()
    for move in moves:
        @pl.when(move[1])
        def _(move=move):
            halo_copy(move).wait_send()
    store_coadd.wait()
    for store in stores:
        store.wait()


def finish(coadd_in, vert, sides, ends, bands, coadd_out, detection):
    patch = vert.shape[1]
    corner_end = patch + 2 * LANES
    coadd_out[...] = coadd_in[...]
    detection[...] = (
        dot(vert[...], bands[:patch, :])
        + dot(sides[...], bands[corner_end:corner_end + 2 * EDGE, :])
        + dot(ends[...], bands[patch:corner_end, :])
    )


def body(rows, n, tiles, coeffs, weights, tile_slot, slot_offset):
    count, size = tiles.shape[1], tiles.shape[2]
    slots = n * CAP
    patch = PATCH
    f32, bf16 = jnp.float32, jnp.bfloat16
    basis = jnp.asarray(band_matrices(size))
    edge_at = np.concatenate([np.arange(-EDGE, 0), np.arange(patch, patch + EDGE)])
    corner_at = np.concatenate([np.arange(-LANES, 0), np.arange(patch, patch + LANES)])
    pick_at = np.concatenate([np.arange(EDGE), np.arange(patch - EDGE, patch)])
    pick = (pick_at[:, None] == np.arange(patch)[None, :]).astype(jnp.bfloat16)
    positions = np.concatenate([np.arange(patch), corner_at, edge_at])
    bands_np = np.concatenate([detect_matrix(positions, patch), pick])
    bands = jnp.asarray(bands_np)

    smem = pl.BlockSpec(memory_space=pltpu.SMEM)
    vmem = pl.BlockSpec(memory_space=pltpu.VMEM)
    anyspace = pl.BlockSpec(memory_space=pl.ANY)
    dma = pltpu.SemaphoreType.DMA
    parts = pl.pallas_call(
        functools.partial(kernel, rows, n),
        out_shape=[
            jax.ShapeDtypeStruct((patch, patch), f32),
            jax.ShapeDtypeStruct((patch, patch), bf16),
            jax.ShapeDtypeStruct((patch, 2 * EDGE), bf16),
            jax.ShapeDtypeStruct((patch, 2 * LANES), bf16),
        ],
        in_specs=[smem] * 2 + [vmem] * 2 + [anyspace] * 4,
        out_specs=[anyspace] * 4,
        scratch_shapes=[
            pltpu.VMEM((count, size, size), bf16),
            pltpu.VMEM((count, NB, size, size), bf16),
            pltpu.VMEM((NB * size, size), bf16),
            pltpu.VMEM(bands_np.shape, bf16),
            pltpu.VMEM((slots // 2, size, size), bf16),
            pltpu.VMEM((slots, size, size), bf16),
            pltpu.VMEM((slots // 2, size, size), bf16),
            pltpu.VMEM((slots // 2, size, size), bf16),
            pltpu.VMEM((n, 8, LANES), f32),
            pltpu.VMEM((n, 8, LANES), f32),
            pltpu.VMEM((2 * slots, LANES), jnp.int32),
            pltpu.VMEM((2, 2 * slots, LANES), jnp.int32),
            pltpu.VMEM((patch, patch), f32),
            pltpu.VMEM((patch, patch), f32),
            pltpu.VMEM((patch, patch), f32),
            pltpu.VMEM((2, patch, patch), bf16),
            pltpu.VMEM((patch, patch), bf16),
            pltpu.VMEM((slots, patch), f32),
            pltpu.VMEM((slots, patch), f32),
            pltpu.VMEM((patch, patch), bf16),
            pltpu.VMEM((2 * EDGE, patch), bf16),
            pltpu.VMEM((2 * EDGE, patch), bf16),
            pltpu.VMEM((2 * EDGE, patch), bf16),
            pltpu.VMEM((2 * EDGE, 2 * LANES), bf16),
            pltpu.VMEM((patch, patch), bf16),
            pltpu.VMEM((patch, 2 * EDGE), bf16),
            pltpu.VMEM((patch, 2 * LANES), bf16),
            dma((8,)),
            dma((slots // 2,)),
            dma((slots,)),
            dma((slots // 2,)),
            dma((slots // 2,)),
            dma((n,)),
            dma((n,)),
            dma((1,)),
            dma((2,)),
            dma((2,)),
            dma((1,)),
            dma((8,)),
            dma((8,)),
        ],
        compiler_params=pltpu.CompilerParams(
            collective_id=0, has_side_effects=True, vmem_limit_bytes=VMEM_LIMIT
        ),
        name="coadd",
    )(
        tile_slot, slot_offset, tile_slot, weights, tiles[0], coeffs[0], basis, bands,
    )
    strip = patch // 2

    def strips(columns):
        return pl.BlockSpec((strip, columns), lambda i: (i, 0))

    return tuple(pl.pallas_call(
        finish,
        grid=(patch // strip,),
        out_shape=[jax.ShapeDtypeStruct((patch, patch), f32)] * 2,
        in_specs=[strips(patch), strips(patch), strips(2 * EDGE), strips(2 * LANES),
                  pl.BlockSpec(bands_np.shape, lambda i: (0, 0))],
        out_specs=[strips(patch)] * 2,
        compiler_params=pltpu.CompilerParams(vmem_limit_bytes=VMEM_LIMIT),
        name="finish",
    )(*parts, bands))


def solution(mesh):
    in_specs = (
        P("skyy", "skyx", None, None),
        P("skyy", "skyx", None, None, None),
        P("skyy", "skyx"),
        P("skyy", "skyx"),
        P(None, "skyy", "skyx"),
    )
    out_specs = (P("skyy", "skyx"), P("skyy", "skyx"))
    return jax.shard_map(
        functools.partial(body, mesh.shape["skyy"], mesh.shape["skyx"]),
        mesh=mesh, in_specs=in_specs, out_specs=out_specs, check_vma=False,
    )
```
